512 devices in a mesh: seq: 128 (over y, x, z_hi), tp: 4 (over z_lo, core).
Axes of the slice: x: 4, y: 8, z: 8 (z_hi: 4, z_lo: 2; z = z_hi * 2 + z_lo), core: 2. Of those that a mesh axis runs over, the one named last changes fastest.
Arguments:
- targets: bfloat16 [131072, 2048], P('seq', 'tp'), may hold values from -6 to 6
- w_query: bfloat16 [2048, 1024], P(None, 'tp'), may hold values from -0.125 to 0.125
- w_gate: bfloat16 [2048, 1024], P(None, 'tp'), may hold values from -0.125 to 0.125
- norm_gain: float32 [1024], P('tp'), may hold values from 0.25 to 1.75
- hist_keys: bfloat16 [131072, 1024], P('seq', 'tp'), may hold values from -6 to 6
- hist_values: bfloat16 [131072, 1024], P('seq', 'tp')
- user_offset: int32 [2048], P('seq'), may hold values from 0 to 131071, as said below
- user_length: int32 [2048], P('seq'), may hold values from 16 to 2048
- target_user: int32 [131072], P('seq'), may hold values from 0 to 2047, as said below
Outputs:
- scored: bfloat16 [131072, 1024], P('seq', 'tp')
The draws below stay inside these ranges and needn't reach their ends.
Inputs may be any that keep to these rules, and one draw needn't show every extreme that they name: `user_offset`: the users of seq index i are users i * 16 to (i + 1) * 16 - 1; each such user's offset lies in history positions i * 1024 to (i + 1) * 1024 - 1. A history may run past position 131071 and continue at position 0. `target_user`: target items of seq index i belong to users of seq index i.
All inputs are finite; a program needn't handle non-finite values.
Results may differ from the reference program's by a relative error of at most 0.0058.
Values may be sent and summed in bfloat16 or wider, within the bound.
No kernel may reach another device: no remote copies, remote signals or barrier semaphores. Data moves between devices by JAX's collectives and lax.ppermute only.
A program may use at most 64 MiB of HBM per device.

```python
import math
import jax
import jax.numpy as jnp
from jax import lax

D = 2048
HEADS = 8
HDIM = 128
SPAN = 2
U_DEV = 16
TGT_DEV = 1024
HIST_DEV = 1024
HQ = 1024
TARGETS = 131072
HIST = 131072
USERS = 2048
MAXLEN = 2048
MINLEN = 16
N_SEQ = 128


def draw_hist_values(key, part):
    first, second = jax.random.split(key)
    columns = jnp.exp(jax.random.uniform(first, (1, HQ), jnp.float32, 0.0, math.log(10.0)))
    base = jax.random.normal(second, (HIST, HQ), jnp.float32)
    return (base * columns).astype(jnp.bfloat16)


def draw_user_offset(key, part):
    owner = jnp.arange(USERS, dtype=jnp.int32) // U_DEV
    local = jax.random.randint(jax.random.fold_in(key, 11), (USERS,), 0, HIST_DEV, dtype=jnp.int32)
    offsets = owner * HIST_DEV + local
    return offsets.at[USERS - 1].set(HIST - 1)


def draw_user_length(key, part):
    kinds = jax.random.randint(jax.random.fold_in(key, 21), (USERS // U_DEV,), 0, 3, dtype=jnp.int32)
    capped = jnp.where(kinds == 0, max(HIST_DEV // 8, MINLEN), jnp.where(kinds == 1, HIST_DEV, MAXLEN))
    capped = jnp.repeat(capped, U_DEV)
    extra = jax.random.randint(jax.random.fold_in(key, 22), (USERS,), 0, capped - MINLEN + 1, dtype=jnp.int32)
    lengths = MINLEN + extra
    lengths = lengths.at[USERS - 1].set(MAXLEN)
    return lengths.at[USERS - 2].set(MINLEN)


def draw_target_user(key, part):
    places = jnp.arange(TARGETS, dtype=jnp.int32)
    owner = places // TGT_DEV
    local = jax.random.randint(jax.random.fold_in(key, 31), (TARGETS,), 0, U_DEV, dtype=jnp.int32)
    local = jnp.where(places % TGT_DEV == 0, U_DEV - 1, local)
    local = jnp.where(places % TGT_DEV == 1, 0, local)
    return owner * U_DEV + local


def levels(stream_key, extent, cuts, least, high):
    factor_of, own = 1.0, jax.random.fold_in(stream_key, 6)
    for position, shards_of in cuts:
        steps = jnp.exp(jax.random.uniform(jax.random.fold_in(own, position), (shards_of,), jnp.float32, least / len(cuts), high / len(cuts)))
        factor_of = factor_of * jnp.repeat(steps, extent[position] // shards_of).reshape([-1 if axis == position else 1 for axis in range(len(extent))])
    return factor_of


def scatter_about(stream_key, dims, scale, reach, shards=(), kind=jnp.bfloat16):
    factor_of = levels(stream_key, dims, shards, -0.22, 0.18) if shards else 1.0
    drawn = jax.random.normal(stream_key, dims, jnp.float32) * scale * factor_of
    return jnp.minimum(jnp.maximum(drawn, -reach), reach).astype(kind)


def setup_inputs(seed: int = 0) -> dict:
    splits = jax.random.split(jax.random.key(seed), 10)
    return {
        "targets": scatter_about(splits[0], (TARGETS, D), 1.0, 6.0, ((0, 128), (1, 4))),
        "w_query": scatter_about(splits[1], (D, HQ), D ** -0.5, 0.125, ((1, 4),)),
        "w_gate": scatter_about(splits[2], (D, HQ), D ** -0.5, 0.125, ((1, 4),)),
        "norm_gain": jnp.clip(1.0 + 0.15 * jax.random.normal(splits[3], (HQ,), jnp.float32), 0.25, 1.75),
        "hist_keys": scatter_about(splits[4], (HIST, HQ), 1.0, 6.0, ((0, 128), (1, 4))),
        "hist_values": draw_hist_values(jax.random.fold_in(splits[9], 71), 0),
        "user_offset": draw_user_offset(jax.random.fold_in(splits[9], 71), 0),
        "user_length": draw_user_length(jax.random.fold_in(splits[9], 71), 0),
        "target_user": draw_target_user(jax.random.fold_in(splits[9], 71), 0),
    }


def reference(targets, w_query, w_gate, norm_gain, hist_keys, hist_values, user_offset, user_length, target_user):
    width = SPAN * HIST_DEV
    ext_keys = jnp.concatenate([hist_keys, hist_keys[:width]], axis=0)
    ext_values = jnp.concatenate([hist_values, hist_values[:width]], axis=0)
    window = (SPAN + 1) * HIST_DEV
    scale = HDIM ** (-0.5)

    def one_block(index):
        index = index.astype(jnp.int32)
        tstart = (index * TGT_DEV).astype(jnp.int32)
        hstart = (index * HIST_DEV).astype(jnp.int32)
        rows = lax.dynamic_slice_in_dim(targets, tstart, TGT_DEV, 0)
        users = lax.dynamic_slice_in_dim(target_user, tstart, TGT_DEV, 0)
        query = jnp.dot(rows, w_query, preferred_element_type=jnp.float32).astype(jnp.bfloat16)
        gate = jax.nn.silu(jnp.dot(rows, w_gate, preferred_element_type=jnp.float32))
        offsets = user_offset[users]
        lengths = user_length[users]
        keys = lax.dynamic_slice_in_dim(ext_keys, hstart, window, 0)
        values = lax.dynamic_slice_in_dim(ext_values, hstart, window, 0)
        places = (hstart + jnp.arange(window, dtype=jnp.int32)) % HIST
        relative = (places[None, :] - offsets[:, None]) % HIST
        inside = relative < lengths[:, None]
        qheads = query.astype(jnp.float32).reshape(TGT_DEV, HEADS, HDIM)
        kheads = keys.astype(jnp.float32).reshape(window, HEADS, HDIM)
        vheads = values.astype(jnp.float32).reshape(window, HEADS, HDIM)
        scores = jnp.einsum('thd,phd->thp', qheads, kheads) * scale
        weight = jnp.where(inside[:, None, :], jax.nn.silu(scores), 0.0).astype(jnp.bfloat16)
        attended = jnp.einsum('thp,phd->thd', weight.astype(jnp.float32), vheads).reshape(TGT_DEV, HQ)
        mean = lax.optimization_barrier(jnp.sum(attended, axis=1, keepdims=True)) / HQ
        var = lax.optimization_barrier(jnp.sum(attended * attended, axis=1, keepdims=True)) / HQ - mean * mean
        normed = (attended - mean) / jnp.sqrt(var + 1e-05)
        return (normed * norm_gain[None, :] * gate).astype(jnp.bfloat16)
    blocks = lax.map(one_block, jnp.arange(N_SEQ, dtype=jnp.int32))
    return blocks.reshape(TARGETS, HQ)
```

```python
import functools

import jax
import jax.numpy as jnp
from jax import lax
from jax.experimental import pallas as pl
from jax.experimental.pallas import tpu as pltpu
from jax.sharding import PartitionSpec as P

HDIM = 128
U_DEV = 16
HQ = 1024
Z_HI = 4
LANES = 128
DOWN_ROWS = 640
VMEM = pl.BlockSpec(memory_space=pltpu.VMEM)
SMEM = pl.BlockSpec(memory_space=pltpu.SMEM)
PARAMS = pltpu.CompilerParams(vmem_limit_bytes=40 * 2**20)


def ring_perms(n_seq):
    down = [(i, (i - 1) % n_seq) for i in range(n_seq)]
    up = []
    for stage in range(3):
        pairs = []
        for i in range(n_seq):
            column, z = divmod(i, Z_HI)
            origin = (z - stage) % Z_HI
            shift = 0
            if stage == 1 and origin == 0:
                shift = -1
            if stage == 1 and origin == 1:
                shift = -1
            if stage == 2 and origin == 1:
                shift = 1
            target = (column + shift) % (n_seq // Z_HI) * Z_HI + (z + 1) % Z_HI
            pairs.append((i, target))
        up.append(pairs)
    return down, up


def windows_kernel(seq_ref, offset_ref, length_ref, user_ref, start_ref, end_ref):
    first_user = seq_ref[0] * U_DEV
    first_row = seq_ref[0] * seq_ref[1]
    user = user_ref[...] - first_user
    start = jnp.zeros_like(user)
    end = jnp.zeros_like(user)
    for u in range(U_DEV):
        mine = user == u
        low = offset_ref[u] - first_row
        start = jnp.where(mine, low, start)
        end = jnp.where(mine, low + length_ref[u], end)
    for group in range(user.shape[0]):
        rows = slice(group * LANES, (group + 1) * LANES)
        start_ref[rows, :] = jnp.broadcast_to(start[group : group + 1], (LANES, LANES)).T
        end_ref[rows, :] = jnp.broadcast_to(end[group : group + 1], (LANES, LANES)).T


def windows(seq_info, user_offset, user_length, target_user):
    rows = target_user.shape[0]
    wide = jax.ShapeDtypeStruct((rows, LANES), jnp.int32)
    return pl.pallas_call(
        windows_kernel,
        out_shape=(wide, wide),
        in_specs=[SMEM, SMEM, SMEM, VMEM],
        out_specs=(VMEM, VMEM),
        compiler_params=PARAMS,
    )(seq_info, user_offset, user_length, target_user.reshape(rows // LANES, LANES))


def project_kernel(order_ref, a_ref, b_ref, wqa, wqb, wga, wgb, *refs, last):
    a, b = a_ref[...], b_ref[...]
    dot = functools.partial(jnp.dot, preferred_element_type=jnp.float32)
    query = dot(a, wqa[...]) + dot(b, wqb[...])
    gate = dot(a, wga[...]) + dot(b, wgb[...])
    width = query.shape[1]
    if last:
        partial_ref, query_ref, gate_ref = refs
        query_ref[...] = (query + partial_ref[:, :width]).astype(jnp.bfloat16)
        gate_ref[...] = jax.nn.silu(gate + partial_ref[:, width:])
    else:
        (partial_ref,) = refs
        partial_ref[:, :width] = query
        partial_ref[:, width:] = gate


def project(order, a, b, w_query, w_gate, partial=None):
    rows, depth = a.shape
    width = w_query.shape[1]
    tile = 256
    feature = pl.BlockSpec((tile, depth), lambda i, order: (i, 0))
    first = pl.BlockSpec((depth, width), lambda i, order: (order[0], 0))
    second = pl.BlockSpec((depth, width), lambda i, order: (order[1], 0))
    sums = pl.BlockSpec((tile, 2 * width), lambda i, order: (i, 0))
    half = pl.BlockSpec((tile, width), lambda i, order: (i, 0))
    in_specs = [feature, feature, first, second, first, second]
    args = [a, b, w_query, w_query, w_gate, w_gate]
    if partial is None:
        out_specs = sums
        out_shape = jax.ShapeDtypeStruct((rows, 2 * width), jnp.float32)
    else:
        in_specs.append(sums)
        args.append(partial)
        out_specs = (half, half)
        out_shape = (
            jax.ShapeDtypeStruct((rows, width), jnp.bfloat16),
            jax.ShapeDtypeStruct((rows, width), jnp.float32),
        )
    return pl.pallas_call(
        functools.partial(project_kernel, last=partial is not None),
        out_shape=out_shape,
        grid_spec=pltpu.PrefetchScalarGridSpec(
            num_scalar_prefetch=1, grid=(rows // tile,), in_specs=in_specs, out_specs=out_specs
        ),
        compiler_params=PARAMS,
        cost_estimate=pl.CostEstimate(
            flops=8 * rows * depth * width, bytes_accessed=8 * rows * depth, transcendentals=0
        ),
    )(order, *args)


def weigh(query, keys, values, start, end, place, total):
    rows = query.shape[0]
    for at in range(0, keys.shape[0], 256):
        size = min(256, keys.shape[0] - at)
        scores = lax.dot_general(
            query, keys[at : at + size], (((1,), (1,)), ((), ())), preferred_element_type=jnp.float32
        )
        columns = []
        for lane in range(0, size, LANES):
            half = scores[:, lane : lane + LANES] * (0.5 * HDIM**-0.5)
            weight = half * jnp.tanh(half) + half
            position = lax.broadcasted_iota(jnp.int32, (rows, LANES), 1) + (place + at + lane)
            inside = position < end
            if start is not None:
                inside = inside & (position >= start)
            columns.append(jnp.where(inside, weight, 0.0).astype(jnp.bfloat16))
        total = total + jnp.dot(
            jnp.concatenate(columns, axis=1), values[at : at + size], preferred_element_type=jnp.float32
        )
    return total


def own_kernel(query_ref, start_ref, end_ref, key_ref, value_ref, out_ref):
    for head in range(query_ref.shape[1] // HDIM):
        cols = slice(head * HDIM, (head + 1) * HDIM)
        zero = jnp.zeros((query_ref.shape[0], HDIM), jnp.float32)
        out_ref[:, cols] = weigh(
            query_ref[:, cols], key_ref[:, cols], value_ref[:, cols], start_ref[...], end_ref[...], 0, zero
        )


def next_kernel(query_ref, end_ref, pair_ref, total_ref, out_ref, *stats, place):
    parts = []
    for head in range(query_ref.shape[1] // HDIM):
        cols = slice(head * HDIM, (head + 1) * HDIM)
        part = weigh(
            query_ref[:, cols], pair_ref[0, :, cols], pair_ref[1, :, cols], None, end_ref[...], place,
            total_ref[:, cols],
        )
        out_ref[:, cols] = part
        parts.append(part)
    if stats:
        (stats_ref,) = stats
        plain = functools.reduce(jnp.add, parts)
        square = functools.reduce(jnp.add, [part * part for part in parts])
        for group in range(plain.shape[0] // LANES):
            rows = slice(group * LANES, (group + 1) * LANES)
            stats_ref[0:1, rows] = jnp.sum(plain[rows].T, axis=0, keepdims=True)
            stats_ref[1:2, rows] = jnp.sum(square[rows].T, axis=0, keepdims=True)


def attend_cost(rows, history, width):
    return pl.CostEstimate(
        flops=4 * rows * history * width, bytes_accessed=8 * rows * width, transcendentals=rows * history * 2
    )


def attend_own(query, start, end, keys, values):
    return pl.pallas_call(
        own_kernel,
        out_shape=jax.ShapeDtypeStruct(query.shape, jnp.float32),
        in_specs=[VMEM] * 5,
        out_specs=VMEM,
        compiler_params=PARAMS,
        cost_estimate=attend_cost(query.shape[0], *keys.shape),
    )(query, start, end, keys, values)


def attend_next(query, end, pair, total, place, last=False):
    out_shape = [jax.ShapeDtypeStruct(query.shape, jnp.float32)]
    if last:
        out_shape.append(jax.ShapeDtypeStruct((2, query.shape[0]), jnp.float32))
    out = pl.pallas_call(
        functools.partial(next_kernel, place=place),
        out_shape=out_shape,
        in_specs=[VMEM] * 4,
        out_specs=[VMEM] * len(out_shape),
        input_output_aliases={3: 0},
        compiler_params=PARAMS,
        cost_estimate=attend_cost(query.shape[0], *pair.shape[1:]),
    )(query, end, pair, total)
    return out if last else out[0]


def body(
    targets,
    w_query,
    w_gate,
    norm_gain,
    hist_keys,
    hist_values,
    user_offset,
    user_length,
    target_user,
):
    hist_rows = hist_keys.shape[0]
    down, up = ring_perms(lax.axis_size("seq"))
    cut = DOWN_ROWS
    other_chip = [(0, 2), (2, 0), (1, 3), (3, 1)]
    other_core = [(0, 1), (1, 0), (2, 3), (3, 2)]

    pair_a = jnp.stack([hist_keys[:cut], hist_values[:cut]])
    pair_b = jnp.stack([hist_keys[cut:], hist_values[cut:]])
    far = lax.ppermute(targets, "tp", other_chip)
    next_a = lax.ppermute(pair_a, "seq", down)
    up_b = lax.ppermute(pair_b, "seq", up[0])
    near = lax.ppermute(targets, "tp", other_core)
    far_near = lax.ppermute(far, "tp", other_core)
    over_b = lax.ppermute(up_b, "seq", up[1])
    over_a = lax.ppermute(next_a, "seq", down)
    next_b = lax.ppermute(over_b, "seq", up[2])

    me = lax.axis_index("tp").astype(jnp.int32)
    seq_info = jnp.stack([lax.axis_index("seq").astype(jnp.int32), jnp.int32(hist_rows)])
    start, end = windows(seq_info, user_offset, user_length, target_user)
    partial = project(jnp.stack([me, me ^ 1]), targets, near, w_query, w_gate)
    query, gate = project(jnp.stack([me ^ 2, me ^ 3]), far, far_near, w_query, w_gate, partial)

    total = attend_own(query, start, end, hist_keys, hist_values)
    total = attend_next(query, end, next_a, total, hist_rows)
    total = attend_next(query, end, over_b, total, 2 * hist_rows + cut)
    total = attend_next(query, end, over_a, total, 2 * hist_rows)
    attended, stats = attend_next(query, end, next_b, total, hist_rows + cut, last=True)

    sums = lax.psum(stats, "tp") / HQ
    mean = sums[0]
    var = sums[1] - mean * mean
    normed = (attended - mean[:, None]) / jnp.sqrt(var[:, None] + 1e-05)
    return (normed * norm_gain[None, :] * gate).astype(jnp.bfloat16)


def solution(mesh):
    return jax.shard_map(
        body,
        mesh=mesh,
        in_specs=(
            P("seq", "tp"),
            P(None, "tp"),
            P(None, "tp"),
            P("tp"),
            P("seq", "tp"),
            P("seq", "tp"),
            P("seq"),
            P("seq"),
            P("seq"),
        ),
        out_specs=P("seq", "tp"),
        check_vma=False,
    )
```

```python
import functools

import jax
import jax.numpy as jnp
from jax import lax
from jax.experimental import pallas as pl
from jax.experimental.pallas import tpu as pltpu
from jax.sharding import PartitionSpec as P

HDIM = 128
U_DEV = 16
HQ = 1024
Z_HI = 4
LANES = 128
DOWN_ROWS = 640
VMEM = pl.BlockSpec(memory_space=pltpu.VMEM)
SMEM = pl.BlockSpec(memory_space=pltpu.SMEM)
PARAMS = pltpu.CompilerParams(vmem_limit_bytes=40 * 2**20)


def ring_perms(n_seq):
    down = [(i, (i - 1) % n_seq) for i in range(n_seq)]
    up = []
    for stage in range(3):
        pairs = []
        for i in range(n_seq):
            column, z = divmod(i, Z_HI)
            origin = (z - stage) % Z_HI
            shift = 0
            if stage == 1 and origin == 0:
                shift = -1
            if stage == 1 and origin == 1:
                shift = -1
            if stage == 2 and origin == 1:
                shift = 1
            target = (column + shift) % (n_seq // Z_HI) * Z_HI + (z + 1) % Z_HI
            pairs.append((i, target))
        up.append(pairs)
    return down, up


def pack_kernel(key_ref, value_ref, a_ref, b_ref):
    cut = a_ref.shape[1]
    for place, ref in enumerate((key_ref, value_ref)):
        a_ref[place] = ref[:cut]
        b_ref[place] = ref[cut:]


def pack(keys, values, cut):
    rows, width = keys.shape
    return pl.pallas_call(
        pack_kernel,
        out_shape=(
            jax.ShapeDtypeStruct((2, cut, width), keys.dtype),
            jax.ShapeDtypeStruct((2, rows - cut, width), keys.dtype),
        ),
        in_specs=[VMEM] * 2,
        out_specs=(VMEM, VMEM),
        compiler_params=PARAMS,
    )(keys, values)


def windows_kernel(seq_ref, offset_ref, length_ref, user_ref, start_ref, end_ref):
    first_user = seq_ref[0] * U_DEV
    first_row = seq_ref[0] * seq_ref[1]
    user = user_ref[...] - first_user
    start = jnp.zeros_like(user)
    end = jnp.zeros_like(user)
    for u in range(U_DEV):
        mine = user == u
        low = offset_ref[u] - first_row
        start = jnp.where(mine, low, start)
        end = jnp.where(mine, low + length_ref[u], end)
    for group in range(user.shape[0]):
        rows = slice(group * LANES, (group + 1) * LANES)
        start_ref[rows, :] = jnp.broadcast_to(start[group : group + 1], (LANES, LANES)).T
        end_ref[rows, :] = jnp.broadcast_to(end[group : group + 1], (LANES, LANES)).T


def windows(seq_info, user_offset, user_length, target_user):
    rows = target_user.shape[0]
    wide = jax.ShapeDtypeStruct((rows, LANES), jnp.int32)
    return pl.pallas_call(
        windows_kernel,
        out_shape=(wide, wide),
        in_specs=[SMEM, SMEM, SMEM, VMEM],
        out_specs=(VMEM, VMEM),
        compiler_params=PARAMS,
    )(seq_info, user_offset, user_length, target_user.reshape(rows // LANES, LANES))


def project_kernel(order_ref, a_ref, b_ref, wqa, wqb, wga, wgb, *refs, last):
    a, b = a_ref[...], b_ref[...]
    dot = functools.partial(jnp.dot, preferred_element_type=jnp.float32)
    query = dot(a, wqa[...]) + dot(b, wqb[...])
    gate = dot(a, wga[...]) + dot(b, wgb[...])
    width = query.shape[1]
    if last:
        partial_ref, query_ref, gate_ref = refs
        query_ref[...] = (query + partial_ref[:, :width]).astype(jnp.bfloat16)
        gate_ref[...] = jax.nn.silu(gate + partial_ref[:, width:])
    else:
        (partial_ref,) = refs
        partial_ref[:, :width] = query
        partial_ref[:, width:] = gate


def project(order, a, b, w_query, w_gate, partial=None):
    rows, depth = a.shape
    width = w_query.shape[1]
    tile = 256
    feature = pl.BlockSpec((tile, depth), lambda i, order: (i, 0))
    first = pl.BlockSpec((depth, width), lambda i, order: (order[0], 0))
    second = pl.BlockSpec((depth, width), lambda i, order: (order[1], 0))
    sums = pl.BlockSpec((tile, 2 * width), lambda i, order: (i, 0))
    half = pl.BlockSpec((tile, width), lambda i, order: (i, 0))
    in_specs = [feature, feature, first, second, first, second]
    args = [a, b, w_query, w_query, w_gate, w_gate]
    if partial is None:
        out_specs = sums
        out_shape = jax.ShapeDtypeStruct((rows, 2 * width), jnp.float32)
    else:
        in_specs.append(sums)
        args.append(partial)
        out_specs = (half, half)
        out_shape = (
            jax.ShapeDtypeStruct((rows, width), jnp.bfloat16),
            jax.ShapeDtypeStruct((rows, width), jnp.float32),
        )
    return pl.pallas_call(
        functools.partial(project_kernel, last=partial is not None),
        out_shape=out_shape,
        grid_spec=pltpu.PrefetchScalarGridSpec(
            num_scalar_prefetch=1, grid=(rows // tile,), in_specs=in_specs, out_specs=out_specs
        ),
        compiler_params=PARAMS,
        cost_estimate=pl.CostEstimate(
            flops=8 * rows * depth * width, bytes_accessed=8 * rows * depth, transcendentals=0
        ),
    )(order, *args)


def weigh(query, keys, values, start, end, place, total):
    rows = query.shape[0]
    for at in range(0, keys.shape[0], 256):
        size = min(256, keys.shape[0] - at)
        scores = lax.dot_general(
            query, keys[at : at + size], (((1,), (1,)), ((), ())), preferred_element_type=jnp.float32
        )
        columns = []
        for lane in range(0, size, LANES):
            half = scores[:, lane : lane + LANES] * (0.5 * HDIM**-0.5)
            weight = half * jnp.tanh(half) + half
            position = lax.broadcasted_iota(jnp.int32, (rows, LANES), 1) + (place + at + lane)
            inside = position < end
            if start is not None:
                inside = inside & (position >= start)
            columns.append(jnp.where(inside, weight, 0.0).astype(jnp.bfloat16))
        total = total + jnp.dot(
            jnp.concatenate(columns, axis=1), values[at : at + size], preferred_element_type=jnp.float32
        )
    return total


def own_kernel(query_ref, start_ref, end_ref, key_ref, value_ref, out_ref):
    for head in range(query_ref.shape[1] // HDIM):
        cols = slice(head * HDIM, (head + 1) * HDIM)
        zero = jnp.zeros((query_ref.shape[0], HDIM), jnp.float32)
        out_ref[:, cols] = weigh(
            query_ref[:, cols], key_ref[:, cols], value_ref[:, cols], start_ref[...], end_ref[...], 0, zero
        )


def next_kernel(query_ref, end_ref, pair_ref, total_ref, out_ref, *stats, place):
    parts = []
    for head in range(query_ref.shape[1] // HDIM):
        cols = slice(head * HDIM, (head + 1) * HDIM)
        part = weigh(
            query_ref[:, cols], pair_ref[0, :, cols], pair_ref[1, :, cols], None, end_ref[...], place,
            total_ref[:, cols],
        )
        out_ref[:, cols] = part
        parts.append(part)
    if stats:
        (stats_ref,) = stats
        plain = functools.reduce(jnp.add, parts)
        square = functools.reduce(jnp.add, [part * part for part in parts])
        for group in range(plain.shape[0] // LANES):
            rows = slice(group * LANES, (group + 1) * LANES)
            stats_ref[0:1, rows] = jnp.sum(plain[rows].T, axis=0, keepdims=True)
            stats_ref[1:2, rows] = jnp.sum(square[rows].T, axis=0, keepdims=True)


def attend_cost(rows, history, width):
    return pl.CostEstimate(
        flops=4 * rows * history * width, bytes_accessed=8 * rows * width, transcendentals=rows * history * 2
    )


def attend_own(query, start, end, keys, values):
    return pl.pallas_call(
        own_kernel,
        out_shape=jax.ShapeDtypeStruct(query.shape, jnp.float32),
        in_specs=[VMEM] * 5,
        out_specs=VMEM,
        compiler_params=PARAMS,
        cost_estimate=attend_cost(query.shape[0], *keys.shape),
    )(query, start, end, keys, values)


def attend_next(query, end, pair, total, place, last=False):
    out_shape = [jax.ShapeDtypeStruct(query.shape, jnp.float32)]
    if last:
        out_shape.append(jax.ShapeDtypeStruct((2, query.shape[0]), jnp.float32))
    out = pl.pallas_call(
        functools.partial(next_kernel, place=place),
        out_shape=out_shape,
        in_specs=[VMEM] * 4,
        out_specs=[VMEM] * len(out_shape),
        input_output_aliases={3: 0},
        compiler_params=PARAMS,
        cost_estimate=attend_cost(query.shape[0], *pair.shape[1:]),
    )(query, end, pair, total)
    return out if last else out[0]


def body(
    targets,
    w_query,
    w_gate,
    norm_gain,
    hist_keys,
    hist_values,
    user_offset,
    user_length,
    target_user,
):
    hist_rows = hist_keys.shape[0]
    down, up = ring_perms(lax.axis_size("seq"))
    cut = DOWN_ROWS
    other_chip = [(0, 2), (2, 0), (1, 3), (3, 1)]
    other_core = [(0, 1), (1, 0), (2, 3), (3, 2)]

    pair_a, pair_b = pack(hist_keys, hist_values, cut)
    far = lax.ppermute(targets, "tp", other_chip)
    next_a = lax.ppermute(pair_a, "seq", down)
    up_b = lax.ppermute(pair_b, "seq", up[0])
    near = lax.ppermute(targets, "tp", other_core)
    far, up_b = lax.optimization_barrier((far, up_b))
    far_near = lax.ppermute(far, "tp", other_core)
    over_b = lax.ppermute(up_b, "seq", up[1])
    over_a = lax.ppermute(next_a, "seq", down)
    next_b = lax.ppermute(over_b, "seq", up[2])

    me = lax.axis_index("tp").astype(jnp.int32)
    seq_info = jnp.stack([lax.axis_index("seq").astype(jnp.int32), jnp.int32(hist_rows)])
    start, end = windows(seq_info, user_offset, user_length, target_user)
    partial = project(jnp.stack([me, me ^ 1]), targets, near, w_query, w_gate)
    query, gate = project(jnp.stack([me ^ 2, me ^ 3]), far, far_near, w_query, w_gate, partial)

    total = attend_own(query, start, end, hist_keys, hist_values)
    total = attend_next(query, end, next_a, total, hist_rows)
    total = attend_next(query, end, over_b, total, 2 * hist_rows + cut)
    total = attend_next(query, end, over_a, total, 2 * hist_rows)
    attended, stats = attend_next(query, end, next_b, total, hist_rows + cut, last=True)

    sums = lax.psum(stats, "tp") / HQ
    mean = sums[0]
    var = sums[1] - mean * mean
    normed = (attended - mean[:, None]) / jnp.sqrt(var[:, None] + 1e-05)
    return (normed * norm_gain[None, :] * gate).astype(jnp.bfloat16)


def solution(mesh):
    return jax.shard_map(
        body,
        mesh=mesh,
        in_specs=(
            P("seq", "tp"),
            P(None, "tp"),
            P(None, "tp"),
            P("tp"),
            P("seq", "tp"),
            P("seq", "tp"),
            P("seq"),
            P("seq"),
            P("seq"),
        ),
        out_specs=P("seq", "tp"),
        check_vma=False,
    )
```

```python
import functools

import jax
import jax.numpy as jnp
from jax import lax
from jax.experimental import pallas as pl
from jax.experimental.pallas import tpu as pltpu
from jax.sharding import PartitionSpec as P

HDIM = 128
U_DEV = 16
HQ = 1024
Z_HI = 4
LANES = 128
DOWN = (624,)
UP = (400,)
VMEM = pl.BlockSpec(memory_space=pltpu.VMEM)
HBM = pl.BlockSpec(memory_space=pltpu.HBM)
SMEM = pl.BlockSpec(memory_space=pltpu.SMEM)
FULL = pltpu.CompilerParams(vmem_limit_bytes=60 * 2**20)
PARAMS = pltpu.CompilerParams(vmem_limit_bytes=40 * 2**20)


def ring_perms(n_seq):
    down = [(i, (i - 1) % n_seq) for i in range(n_seq)]
    up = []
    for stage in range(3):
        pairs = []
        for i in range(n_seq):
            column, z = divmod(i, Z_HI)
            origin = (z - stage) % Z_HI
            shift = 0
            if stage == 1 and origin == 0:
                shift = -1
            if stage == 1 and origin == 1:
                shift = -1
            if stage == 2 and origin == 1:
                shift = 1
            target = (column + shift) % (n_seq // Z_HI) * Z_HI + (z + 1) % Z_HI
            pairs.append((i, target))
        up.append(pairs)
    return down, up


def pack_kernel(chunks, key_ref, value_ref, *refs):
    outs, sems = refs[:-1], refs[-1]
    copies = []
    for (at, size), out in zip(chunks, outs):
        for place, ref in enumerate((key_ref, value_ref)):
            copies.append(
                pltpu.make_async_copy(ref.at[pl.ds(at, size)], out.at[place], sems.at[len(copies)])
            )
    for copy in copies:
        copy.start()
    for copy in copies:
        copy.wait()


def pack(keys, values, chunks):
    width = keys.shape[1]
    return pl.pallas_call(
        functools.partial(pack_kernel, chunks),
        out_shape=[jax.ShapeDtypeStruct((2, size, width), keys.dtype) for _, size in chunks],
        in_specs=[HBM] * 2,
        out_specs=[VMEM] * len(chunks),
        scratch_shapes=[pltpu.SemaphoreType.DMA((2 * len(chunks),))],
        cost_estimate=pl.CostEstimate(flops=1, bytes_accessed=1, transcendentals=0),
        compiler_params=FULL,
    )(keys, values)


def windows_kernel(seq_ref, offset_ref, length_ref, user_ref, start_ref, end_ref):
    first_user = seq_ref[0] * U_DEV
    first_row = seq_ref[0] * seq_ref[1]
    user = user_ref[...] - first_user
    start = jnp.zeros_like(user)
    end = jnp.zeros_like(user)
    for u in range(U_DEV):
        mine = user == u
        low = offset_ref[u] - first_row
        start = jnp.where(mine, low, start)
        end = jnp.where(mine, low + length_ref[u], end)
    for group in range(user.shape[0]):
        rows = slice(group * LANES, (group + 1) * LANES)
        start_ref[rows, :] = jnp.broadcast_to(start[group : group + 1], (LANES, LANES)).T
        end_ref[rows, :] = jnp.broadcast_to(end[group : group + 1], (LANES, LANES)).T


def windows(seq_info, user_offset, user_length, target_user):
    rows = target_user.shape[0]
    wide = jax.ShapeDtypeStruct((rows, LANES), jnp.int32)
    return pl.pallas_call(
        windows_kernel,
        out_shape=(wide, wide),
        in_specs=[SMEM, SMEM, SMEM, VMEM],
        out_specs=(VMEM, VMEM),
        cost_estimate=pl.CostEstimate(flops=20000000000, bytes_accessed=1, transcendentals=0),
        compiler_params=FULL,
    )(seq_info, user_offset, user_length, target_user.reshape(rows // LANES, LANES))


def project_kernel(order_ref, *refs):
    features, refs = [ref[...] for ref in refs[:4]], refs[4:]
    sums = []
    for weights in (refs[0:4], refs[4:8]):
        dots = [
            jnp.dot(feature, weight[...], preferred_element_type=jnp.float32)
            for feature, weight in zip(features, weights)
        ]
        sums.append(dots[0] + dots[1] + (dots[2] + dots[3]))
    query_ref, gate_ref = refs[8:]
    query_ref[...] = sums[0].astype(jnp.bfloat16)
    gate_ref[...] = jax.nn.silu(sums[1])


def project(order, pieces, w_query, w_gate, flops=1):
    rows, depth = pieces[0].shape
    width = w_query.shape[1]
    tile = 256
    feature = pl.BlockSpec((tile, depth), lambda i, order: (i, 0))
    weight = [pl.BlockSpec((depth, width), lambda i, order, k=k: (order[k], 0)) for k in range(4)]
    half = pl.BlockSpec((tile, width), lambda i, order: (i, 0))
    return pl.pallas_call(
        project_kernel,
        out_shape=(
            jax.ShapeDtypeStruct((rows, width), jnp.bfloat16),
            jax.ShapeDtypeStruct((rows, width), jnp.float32),
        ),
        grid_spec=pltpu.PrefetchScalarGridSpec(
            num_scalar_prefetch=1,
            grid=(rows // tile,),
            in_specs=[feature] * 4 + weight * 2,
            out_specs=(half, half),
        ),
        compiler_params=PARAMS,
        cost_estimate=pl.CostEstimate(flops=flops, bytes_accessed=1, transcendentals=0),
    )(order, *pieces, *[w_query] * 4, *[w_gate] * 4)


def weigh(query, keys, values, start, end, place, total):
    rows = query.shape[0]
    for at in range(0, keys.shape[0], 256):
        size = min(256, keys.shape[0] - at)
        scores = lax.dot_general(
            query, keys[at : at + size], (((1,), (1,)), ((), ())), preferred_element_type=jnp.float32
        )
        columns = []
        for lane in range(0, size, LANES):
            lanes = min(LANES, size - lane)
            half = scores[:, lane : lane + lanes] * (0.5 * HDIM**-0.5)
            weight = half * jnp.tanh(half) + half
            position = lax.broadcasted_iota(jnp.int32, (rows, lanes), 1) + (place + at + lane)
            inside = position < end[:, :lanes]
            if start is not None:
                inside = inside & (position >= start[:, :lanes])
            columns.append(jnp.where(inside, weight, 0.0).astype(jnp.bfloat16))
        total = total + jnp.dot(
            jnp.concatenate(columns, axis=1), values[at : at + size], preferred_element_type=jnp.float32
        )
    return total


def own_kernel(query_ref, start_ref, end_ref, key_ref, value_ref, out_ref):
    for head in range(query_ref.shape[1] // HDIM):
        cols = slice(head * HDIM, (head + 1) * HDIM)
        zero = jnp.zeros((query_ref.shape[0], HDIM), jnp.float32)
        out_ref[:, cols] = weigh(
            query_ref[:, cols], key_ref[:, cols], value_ref[:, cols], start_ref[...], end_ref[...], 0, zero
        )


def next_kernel(query_ref, end_ref, *refs, places):
    pairs, (total_ref, out_ref, *stats) = refs[: len(places)], refs[len(places) :]
    parts = []
    for head in range(query_ref.shape[1] // HDIM):
        cols = slice(head * HDIM, (head + 1) * HDIM)
        part = total_ref[:, cols]
        for place, pair_ref in zip(places, pairs):
            part = weigh(
                query_ref[:, cols], pair_ref[0, :, cols], pair_ref[1, :, cols], None, end_ref[...], place, part
            )
        out_ref[:, cols] = part
        parts.append(part)
    if stats:
        (stats_ref,) = stats
        plain = functools.reduce(jnp.add, parts)
        square = functools.reduce(jnp.add, [part * part for part in parts])
        for group in range(plain.shape[0] // LANES):
            rows = slice(group * LANES, (group + 1) * LANES)
            stats_ref[0:1, rows] = jnp.sum(plain[rows].T, axis=0, keepdims=True)
            stats_ref[1:2, rows] = jnp.sum(square[rows].T, axis=0, keepdims=True)


def attend_cost(rows, history, width):
    return pl.CostEstimate(flops=1, bytes_accessed=1, transcendentals=0)


def attend_own(query, start, end, keys, values, flops=1):
    return pl.pallas_call(
        own_kernel,
        out_shape=jax.ShapeDtypeStruct(query.shape, jnp.float32),
        in_specs=[VMEM] * 5,
        out_specs=VMEM,
        compiler_params=PARAMS,
        cost_estimate=pl.CostEstimate(flops=flops, bytes_accessed=1, transcendentals=0),
    )(query, start, end, keys, values)


def attend_next(query, end, chunks, total, last=False, flops=1):
    pairs, places = zip(*chunks)
    out_shape = [jax.ShapeDtypeStruct(query.shape, jnp.float32)]
    if last:
        out_shape.append(jax.ShapeDtypeStruct((2, query.shape[0]), jnp.float32))
    history = sum(pair.shape[1] for pair in pairs)
    out = pl.pallas_call(
        functools.partial(next_kernel, places=places),
        out_shape=out_shape,
        in_specs=[VMEM] * (3 + len(pairs)),
        out_specs=[VMEM] * len(out_shape),
        input_output_aliases={2 + len(pairs): 0},
        compiler_params=PARAMS,
        cost_estimate=pl.CostEstimate(flops=flops, bytes_accessed=1, transcendentals=0),
    )(query, end, *pairs, total)
    return out if last else out[0]


def after(array, *others):
    return lax.optimization_barrier((array, *others))[0]


def body(
    targets,
    w_query,
    w_gate,
    norm_gain,
    hist_keys,
    hist_values,
    user_offset,
    user_length,
    target_user,
):
    hist_rows = hist_keys.shape[0]
    down, up = ring_perms(lax.axis_size("seq"))
    other_chip = [(0, 2), (2, 0), (1, 3), (3, 1)]
    other_core = [(0, 1), (1, 0), (2, 3), (3, 2)]
    sizes = DOWN + UP
    at = [sum(sizes[:i]) for i in range(len(sizes))]
    chunks = tuple(zip(at, sizes))

    me = lax.axis_index("tp").astype(jnp.int32)
    seq_info = jnp.stack([lax.axis_index("seq").astype(jnp.int32), jnp.int32(hist_rows)])
    start, end = windows(seq_info, user_offset, user_length, target_user)
    a, b = pack(hist_keys, hist_values, chunks)
    far = lax.ppermute(targets, "tp", other_chip)
    b1 = lax.ppermute(b, "seq", up[0])
    a1 = lax.ppermute(a, "seq", down)
    far = after(far, b1)
    near = lax.ppermute(after(targets, far), "tp", other_core)
    far_near = lax.ppermute(far, "tp", other_core)
    b2 = lax.ppermute(b1, "seq", up[1])
    a2 = lax.ppermute(a1, "seq", down)
    order = jnp.stack([me, me ^ 1, me ^ 2, me ^ 3])
    query, gate = project(order, (targets, near, far, far_near), w_query, w_gate, flops=500000000)
    total = attend_own(query, start, end, hist_keys, hist_values, flops=1000000000)
    b2 = after(b2, query)
    b3 = lax.ppermute(b2, "seq", up[2])
    one, two = hist_rows, 2 * hist_rows
    total = attend_next(query, end, [(a1, one + at[0])], total, flops=500000000)
    total = attend_next(query, end, [(b2, two + at[1])], total, flops=4000000000)
    total = attend_next(query, end, [(a2, two + at[0])], total, flops=4000000000)
    attended, stats = attend_next(query, end, [(b3, one + at[1])], total, flops=4000000000, last=True)

    sums = lax.psum(stats, "tp") / HQ
    mean = sums[0]
    var = sums[1] - mean * mean
    normed = (attended - mean[:, None]) / jnp.sqrt(var[:, None] + 1e-05)
    return (normed * norm_gain[None, :] * gate).astype(jnp.bfloat16)


def solution(mesh):
    return jax.shard_map(
        body,
        mesh=mesh,
        in_specs=(
            P("seq", "tp"),
            P(None, "tp"),
            P(None, "tp"),
            P("tp"),
            P("seq", "tp"),
            P("seq", "tp"),
            P("seq"),
            P("seq"),
            P("seq"),
        ),
        out_specs=P("seq", "tp"),
        check_vma=False,
    )
```

```python
import functools

import jax
import jax.numpy as jnp
from jax import lax
from jax.experimental import pallas as pl
from jax.experimental.pallas import tpu as pltpu
from jax.sharding import PartitionSpec as P

HDIM = 128
U_DEV = 16
HQ = 1024
Z_HI = 4
LANES = 128
DOWN = (672,)
UP = (352,)
VMEM = pl.BlockSpec(memory_space=pltpu.VMEM)
HBM = pl.BlockSpec(memory_space=pltpu.HBM)
SMEM = pl.BlockSpec(memory_space=pltpu.SMEM)
FULL = pltpu.CompilerParams(vmem_limit_bytes=60 * 2**20)
PARAMS = pltpu.CompilerParams(vmem_limit_bytes=40 * 2**20)


def ring_perms(n_seq):
    down = [(i, (i - 1) % n_seq) for i in range(n_seq)]
    up = []
    for stage in range(3):
        pairs = []
        for i in range(n_seq):
            column, z = divmod(i, Z_HI)
            origin = (z - stage) % Z_HI
            shift = 0
            if stage == 1 and origin == 0:
                shift = -1
            if stage == 1 and origin == 1:
                shift = -1
            if stage == 2 and origin == 1:
                shift = 1
            target = (column + shift) % (n_seq // Z_HI) * Z_HI + (z + 1) % Z_HI
            pairs.append((i, target))
        up.append(pairs)
    return down, up


def pack_kernel(chunks, key_ref, value_ref, *refs):
    outs, sems = refs[:-1], refs[-1]
    copies = []
    for (at, size), out in zip(chunks, outs):
        for place, ref in enumerate((key_ref, value_ref)):
            copies.append(
                pltpu.make_async_copy(ref.at[pl.ds(at, size)], out.at[place], sems.at[len(copies)])
            )
    for copy in copies:
        copy.start()
    for copy in copies:
        copy.wait()


def pack(keys, values, chunks):
    width = keys.shape[1]
    return pl.pallas_call(
        functools.partial(pack_kernel, chunks),
        out_shape=[jax.ShapeDtypeStruct((2, size, width), keys.dtype) for _, size in chunks],
        in_specs=[HBM] * 2,
        out_specs=[VMEM] * len(chunks),
        scratch_shapes=[pltpu.SemaphoreType.DMA((2 * len(chunks),))],
        compiler_params=FULL,
    )(keys, values)


def windows_kernel(seq_ref, offset_ref, length_ref, user_ref, start_ref, end_ref):
    first_user = seq_ref[0] * U_DEV
    first_row = seq_ref[0] * seq_ref[1]
    user = user_ref[...] - first_user
    start = jnp.zeros_like(user)
    end = jnp.zeros_like(user)
    for u in range(U_DEV):
        mine = user == u
        low = offset_ref[u] - first_row
        start = jnp.where(mine, low, start)
        end = jnp.where(mine, low + length_ref[u], end)
    for group in range(user.shape[0]):
        rows = slice(group * LANES, (group + 1) * LANES)
        start_ref[rows, :] = jnp.broadcast_to(start[group : group + 1], (LANES, LANES)).T
        end_ref[rows, :] = jnp.broadcast_to(end[group : group + 1], (LANES, LANES)).T


def windows(seq_info, user_offset, user_length, target_user):
    rows = target_user.shape[0]
    wide = jax.ShapeDtypeStruct((rows, LANES), jnp.int32)
    return pl.pallas_call(
        windows_kernel,
        out_shape=(wide, wide),
        in_specs=[SMEM, SMEM, SMEM, VMEM],
        out_specs=(VMEM, VMEM),
        compiler_params=PARAMS,
    )(seq_info, user_offset, user_length, target_user.reshape(rows // LANES, LANES))


def project_kernel(order_ref, a_ref, b_ref, wqa, wqb, wga, wgb, *refs, last):
    a, b = a_ref[...], b_ref[...]
    dot = functools.partial(jnp.dot, preferred_element_type=jnp.float32)
    query = dot(a, wqa[...]) + dot(b, wqb[...])
    gate = dot(a, wga[...]) + dot(b, wgb[...])
    width = query.shape[1]
    if last:
        partial_ref, query_ref, gate_ref = refs
        query_ref[...] = (query + partial_ref[:, :width]).astype(jnp.bfloat16)
        gate_ref[...] = jax.nn.silu(gate + partial_ref[:, width:])
    else:
        (partial_ref,) = refs
        partial_ref[:, :width] = query
        partial_ref[:, width:] = gate


def project(order, a, b, w_query, w_gate, partial=None):
    rows, depth = a.shape
    width = w_query.shape[1]
    tile = 256
    feature = pl.BlockSpec((tile, depth), lambda i, order: (i, 0))
    first = pl.BlockSpec((depth, width), lambda i, order: (order[0], 0))
    second = pl.BlockSpec((depth, width), lambda i, order: (order[1], 0))
    sums = pl.BlockSpec((tile, 2 * width), lambda i, order: (i, 0))
    half = pl.BlockSpec((tile, width), lambda i, order: (i, 0))
    in_specs = [feature, feature, first, second, first, second]
    args = [a, b, w_query, w_query, w_gate, w_gate]
    if partial is None:
        out_specs = sums
        out_shape = jax.ShapeDtypeStruct((rows, 2 * width), jnp.float32)
    else:
        in_specs.append(sums)
        args.append(partial)
        out_specs = (half, half)
        out_shape = (
            jax.ShapeDtypeStruct((rows, width), jnp.bfloat16),
            jax.ShapeDtypeStruct((rows, width), jnp.float32),
        )
    return pl.pallas_call(
        functools.partial(project_kernel, last=partial is not None),
        out_shape=out_shape,
        grid_spec=pltpu.PrefetchScalarGridSpec(
            num_scalar_prefetch=1, grid=(rows // tile,), in_specs=in_specs, out_specs=out_specs
        ),
        compiler_params=PARAMS,
        cost_estimate=pl.CostEstimate(
            flops=80 * rows * depth * width // 10, bytes_accessed=8 * rows * depth, transcendentals=0
        ),
    )(order, *args)


def weigh(query, keys, values, start, end, place, total):
    rows = query.shape[0]
    for at in range(0, keys.shape[0], 256):
        size = min(256, keys.shape[0] - at)
        scores = lax.dot_general(
            query, keys[at : at + size], (((1,), (1,)), ((), ())), preferred_element_type=jnp.float32
        )
        columns = []
        for lane in range(0, size, LANES):
            lanes = min(LANES, size - lane)
            half = scores[:, lane : lane + lanes] * (0.5 * HDIM**-0.5)
            weight = half * jnp.tanh(half) + half
            position = lax.broadcasted_iota(jnp.int32, (rows, lanes), 1) + (place + at + lane)
            inside = position < end[:, :lanes]
            if start is not None:
                inside = inside & (position >= start[:, :lanes])
            columns.append(jnp.where(inside, weight, 0.0).astype(jnp.bfloat16))
        total = total + jnp.dot(
            jnp.concatenate(columns, axis=1), values[at : at + size], preferred_element_type=jnp.float32
        )
    return total


def own_kernel(query_ref, start_ref, end_ref, key_ref, value_ref, out_ref):
    for head in range(query_ref.shape[1] // HDIM):
        cols = slice(head * HDIM, (head + 1) * HDIM)
        zero = jnp.zeros((query_ref.shape[0], HDIM), jnp.float32)
        out_ref[:, cols] = weigh(
            query_ref[:, cols], key_ref[:, cols], value_ref[:, cols], start_ref[...], end_ref[...], 0, zero
        )


def next_kernel(query_ref, end_ref, *refs, places):
    pairs, (total_ref, out_ref, *stats) = refs[: len(places)], refs[len(places) :]
    parts = []
    for head in range(query_ref.shape[1] // HDIM):
        cols = slice(head * HDIM, (head + 1) * HDIM)
        part = total_ref[:, cols]
        for place, pair_ref in zip(places, pairs):
            part = weigh(
                query_ref[:, cols], pair_ref[0, :, cols], pair_ref[1, :, cols], None, end_ref[...], place, part
            )
        out_ref[:, cols] = part
        parts.append(part)
    if stats:
        (stats_ref,) = stats
        plain = functools.reduce(jnp.add, parts)
        square = functools.reduce(jnp.add, [part * part for part in parts])
        for group in range(plain.shape[0] // LANES):
            rows = slice(group * LANES, (group + 1) * LANES)
            stats_ref[0:1, rows] = jnp.sum(plain[rows].T, axis=0, keepdims=True)
            stats_ref[1:2, rows] = jnp.sum(square[rows].T, axis=0, keepdims=True)


def attend_cost(rows, history, width):
    return pl.CostEstimate(
        flops=20 * rows * history * width // 10, bytes_accessed=8 * rows * width, transcendentals=rows * history * 2
    )


def attend_own(query, start, end, keys, values):
    return pl.pallas_call(
        own_kernel,
        out_shape=jax.ShapeDtypeStruct(query.shape, jnp.float32),
        in_specs=[VMEM] * 5,
        out_specs=VMEM,
        compiler_params=PARAMS,
        cost_estimate=attend_cost(query.shape[0], *keys.shape),
    )(query, start, end, keys, values)


def attend_next(query, end, chunks, total, last=False):
    pairs, places = zip(*chunks)
    out_shape = [jax.ShapeDtypeStruct(query.shape, jnp.float32)]
    if last:
        out_shape.append(jax.ShapeDtypeStruct((2, query.shape[0]), jnp.float32))
    history = sum(pair.shape[1] for pair in pairs)
    out = pl.pallas_call(
        functools.partial(next_kernel, places=places),
        out_shape=out_shape,
        in_specs=[VMEM] * (3 + len(pairs)),
        out_specs=[VMEM] * len(out_shape),
        input_output_aliases={2 + len(pairs): 0},
        compiler_params=PARAMS,
        cost_estimate=attend_cost(query.shape[0], history, query.shape[1]),
    )(query, end, *pairs, total)
    return out if last else out[0]


def after(array, *others):
    return lax.optimization_barrier((array, *others))[0]


def body(
    targets,
    w_query,
    w_gate,
    norm_gain,
    hist_keys,
    hist_values,
    user_offset,
    user_length,
    target_user,
):
    hist_rows = hist_keys.shape[0]
    down, up = ring_perms(lax.axis_size("seq"))
    other_chip = [(0, 2), (2, 0), (1, 3), (3, 1)]
    other_core = [(0, 1), (1, 0), (2, 3), (3, 2)]
    sizes = DOWN + UP
    at = [sum(sizes[:i]) for i in range(len(sizes))]
    chunks = tuple(zip(at, sizes))

    near = lax.ppermute(targets, "tp", other_core)
    a, b = pack(hist_keys, hist_values, chunks)
    far = lax.ppermute(targets, "tp", other_chip)
    a1 = lax.ppermute(a, "seq", down)
    b1 = lax.ppermute(b, "seq", up[0])
    me = lax.axis_index("tp").astype(jnp.int32)
    seq_info = jnp.stack([lax.axis_index("seq").astype(jnp.int32), jnp.int32(hist_rows)])
    start, end = windows(seq_info, user_offset, user_length, target_user)
    partial = project(jnp.stack([me, me ^ 1]), targets, near, w_query, w_gate)
    far, b1 = lax.optimization_barrier((far, b1))
    far_near = lax.ppermute(far, "tp", other_core)
    b2 = lax.ppermute(b1, "seq", up[1])
    a2 = lax.ppermute(a1, "seq", down)
    query, gate = project(jnp.stack([me ^ 2, me ^ 3]), far, far_near, w_query, w_gate, partial)
    total = attend_own(query, start, end, hist_keys, hist_values)
    b3 = lax.ppermute(b2, "seq", up[2])
    one, two = hist_rows, 2 * hist_rows
    total = attend_next(query, end, [(a1, one + at[0])], total)
    total = attend_next(query, end, [(b2, two + at[1])], total)
    total = attend_next(query, end, [(a2, two + at[0])], total)
    attended, stats = attend_next(query, end, [(b3, one + at[1])], total, last=True)

    sums = lax.psum(stats, "tp") / HQ
    mean = sums[0]
    var = sums[1] - mean * mean
    normed = (attended - mean[:, None]) / jnp.sqrt(var[:, None] + 1e-05)
    return (normed * norm_gain[None, :] * gate).astype(jnp.bfloat16)


def solution(mesh):
    return jax.shard_map(
        body,
        mesh=mesh,
        in_specs=(
            P("seq", "tp"),
            P(None, "tp"),
            P(None, "tp"),
            P("tp"),
            P("seq", "tp"),
            P("seq", "tp"),
            P("seq"),
            P("seq"),
            P("seq"),
        ),
        out_specs=P("seq", "tp"),
        check_vma=False,
    )
```

```python
import functools

import jax
import jax.numpy as jnp
from jax import lax
from jax.experimental import pallas as pl
from jax.experimental.pallas import tpu as pltpu
from jax.sharding import PartitionSpec as P

HDIM = 128
U_DEV = 16
HQ = 1024
Z_HI = 4
LANES = 128
DOWN = (688,)
UP = (336,)
VMEM = pl.BlockSpec(memory_space=pltpu.VMEM)
HBM = pl.BlockSpec(memory_space=pltpu.HBM)
SMEM = pl.BlockSpec(memory_space=pltpu.SMEM)
FULL = pltpu.CompilerParams(vmem_limit_bytes=60 * 2**20)
PARAMS = pltpu.CompilerParams(vmem_limit_bytes=40 * 2**20)


def ring_perms(n_seq):
    down = [(i, (i - 1) % n_seq) for i in range(n_seq)]
    up = []
    for stage in range(3):
        pairs = []
        for i in range(n_seq):
            column, z = divmod(i, Z_HI)
            origin = (z - stage) % Z_HI
            shift = 0
            if stage == 1 and origin == 0:
                shift = -1
            if stage == 1 and origin == 1:
                shift = -1
            if stage == 2 and origin == 1:
                shift = 1
            target = (column + shift) % (n_seq // Z_HI) * Z_HI + (z + 1) % Z_HI
            pairs.append((i, target))
        up.append(pairs)
    return down, up


def pack_kernel(chunks, key_ref, value_ref, *refs):
    outs, sems = refs[:-1], refs[-1]
    copies = []
    for (at, size), out in zip(chunks, outs):
        for place, ref in enumerate((key_ref, value_ref)):
            copies.append(
                pltpu.make_async_copy(ref.at[pl.ds(at, size)], out.at[place], sems.at[len(copies)])
            )
    for copy in copies:
        copy.start()
    for copy in copies:
        copy.wait()


def pack(keys, values, chunks):
    width = keys.shape[1]
    return pl.pallas_call(
        functools.partial(pack_kernel, chunks),
        out_shape=[jax.ShapeDtypeStruct((2, size, width), keys.dtype) for _, size in chunks],
        in_specs=[HBM] * 2,
        out_specs=[VMEM] * len(chunks),
        scratch_shapes=[pltpu.SemaphoreType.DMA((2 * len(chunks),))],
        compiler_params=FULL,
    )(keys, values)


def windows_kernel(seq_ref, offset_ref, length_ref, user_ref, start_ref, end_ref):
    first_user = seq_ref[0] * U_DEV
    first_row = seq_ref[0] * seq_ref[1]
    user = user_ref[...] - first_user
    start = jnp.zeros_like(user)
    end = jnp.zeros_like(user)
    for u in range(U_DEV):
        mine = user == u
        low = offset_ref[u] - first_row
        start = jnp.where(mine, low, start)
        end = jnp.where(mine, low + length_ref[u], end)
    for group in range(user.shape[0]):
        rows = slice(group * LANES, (group + 1) * LANES)
        start_ref[rows, :] = jnp.broadcast_to(start[group : group + 1], (LANES, LANES)).T
        end_ref[rows, :] = jnp.broadcast_to(end[group : group + 1], (LANES, LANES)).T


def windows(seq_info, user_offset, user_length, target_user):
    rows = target_user.shape[0]
    wide = jax.ShapeDtypeStruct((rows, LANES), jnp.int32)
    return pl.pallas_call(
        windows_kernel,
        out_shape=(wide, wide),
        in_specs=[SMEM, SMEM, SMEM, VMEM],
        out_specs=(VMEM, VMEM),
        compiler_params=PARAMS,
    )(seq_info, user_offset, user_length, target_user.reshape(rows // LANES, LANES))


def project_kernel(order_ref, a_ref, b_ref, wqa, wqb, wga, wgb, *refs, last):
    a, b = a_ref[...], b_ref[...]
    dot = functools.partial(jnp.dot, preferred_element_type=jnp.float32)
    query = dot(a, wqa[...]) + dot(b, wqb[...])
    gate = dot(a, wga[...]) + dot(b, wgb[...])
    width = query.shape[1]
    if last:
        partial_ref, query_ref, gate_ref = refs
        query_ref[...] = (query + partial_ref[:, :width]).astype(jnp.bfloat16)
        gate_ref[...] = jax.nn.silu(gate + partial_ref[:, width:])
    else:
        (partial_ref,) = refs
        partial_ref[:, :width] = query
        partial_ref[:, width:] = gate


def project(order, a, b, w_query, w_gate, partial=None):
    rows, depth = a.shape
    width = w_query.shape[1]
    tile = 256
    feature = pl.BlockSpec((tile, depth), lambda i, order: (i, 0))
    first = pl.BlockSpec((depth, width), lambda i, order: (order[0], 0))
    second = pl.BlockSpec((depth, width), lambda i, order: (order[1], 0))
    sums = pl.BlockSpec((tile, 2 * width), lambda i, order: (i, 0))
    half = pl.BlockSpec((tile, width), lambda i, order: (i, 0))
    in_specs = [feature, feature, first, second, first, second]
    args = [a, b, w_query, w_query, w_gate, w_gate]
    if partial is None:
        out_specs = sums
        out_shape = jax.ShapeDtypeStruct((rows, 2 * width), jnp.float32)
    else:
        in_specs.append(sums)
        args.append(partial)
        out_specs = (half, half)
        out_shape = (
            jax.ShapeDtypeStruct((rows, width), jnp.bfloat16),
            jax.ShapeDtypeStruct((rows, width), jnp.float32),
        )
    return pl.pallas_call(
        functools.partial(project_kernel, last=partial is not None),
        out_shape=out_shape,
        grid_spec=pltpu.PrefetchScalarGridSpec(
            num_scalar_prefetch=1, grid=(rows // tile,), in_specs=in_specs, out_specs=out_specs
        ),
        compiler_params=PARAMS,
        cost_estimate=pl.CostEstimate(
            flops=80 * rows * depth * width // 10, bytes_accessed=8 * rows * depth, transcendentals=0
        ),
    )(order, *args)


def weigh(query, keys, values, start, end, place, total):
    rows = query.shape[0]
    for at in range(0, keys.shape[0], 256):
        size = min(256, keys.shape[0] - at)
        scores = lax.dot_general(
            query, keys[at : at + size], (((1,), (1,)), ((), ())), preferred_element_type=jnp.float32
        )
        columns = []
        for lane in range(0, size, LANES):
            lanes = min(LANES, size - lane)
            half = scores[:, lane : lane + lanes] * (0.5 * HDIM**-0.5)
            weight = half * jnp.tanh(half) + half
            position = lax.broadcasted_iota(jnp.int32, (rows, lanes), 1) + (place + at + lane)
            inside = position < end[:, :lanes]
            if start is not None:
                inside = inside & (position >= start[:, :lanes])
            columns.append(jnp.where(inside, weight, 0.0).astype(jnp.bfloat16))
        total = total + jnp.dot(
            jnp.concatenate(columns, axis=1), values[at : at + size], preferred_element_type=jnp.float32
        )
    return total


def own_kernel(query_ref, start_ref, end_ref, key_ref, value_ref, out_ref):
    for head in range(query_ref.shape[1] // HDIM):
        cols = slice(head * HDIM, (head + 1) * HDIM)
        zero = jnp.zeros((query_ref.shape[0], HDIM), jnp.float32)
        out_ref[:, cols] = weigh(
            query_ref[:, cols], key_ref[:, cols], value_ref[:, cols], start_ref[...], end_ref[...], 0, zero
        )


def next_kernel(query_ref, end_ref, *refs, places):
    pairs, (total_ref, out_ref, *stats) = refs[: len(places)], refs[len(places) :]
    parts = []
    for head in range(query_ref.shape[1] // HDIM):
        cols = slice(head * HDIM, (head + 1) * HDIM)
        part = total_ref[:, cols]
        for place, pair_ref in zip(places, pairs):
            part = weigh(
                query_ref[:, cols], pair_ref[0, :, cols], pair_ref[1, :, cols], None, end_ref[...], place, part
            )
        out_ref[:, cols] = part
        parts.append(part)
    if stats:
        (stats_ref,) = stats
        plain = functools.reduce(jnp.add, parts)
        square = functools.reduce(jnp.add, [part * part for part in parts])
        for group in range(plain.shape[0] // LANES):
            rows = slice(group * LANES, (group + 1) * LANES)
            stats_ref[0:1, rows] = jnp.sum(plain[rows].T, axis=0, keepdims=True)
            stats_ref[1:2, rows] = jnp.sum(square[rows].T, axis=0, keepdims=True)


def attend_cost(rows, history, width):
    return pl.CostEstimate(
        flops=20 * rows * history * width // 10, bytes_accessed=8 * rows * width, transcendentals=rows * history * 2
    )


def attend_own(query, start, end, keys, values):
    return pl.pallas_call(
        own_kernel,
        out_shape=jax.ShapeDtypeStruct(query.shape, jnp.float32),
        in_specs=[VMEM] * 5,
        out_specs=VMEM,
        compiler_params=PARAMS,
        cost_estimate=attend_cost(query.shape[0], *keys.shape),
    )(query, start, end, keys, values)


def attend_next(query, end, chunks, total, last=False):
    pairs, places = zip(*chunks)
    out_shape = [jax.ShapeDtypeStruct(query.shape, jnp.float32)]
    if last:
        out_shape.append(jax.ShapeDtypeStruct((2, query.shape[0]), jnp.float32))
    history = sum(pair.shape[1] for pair in pairs)
    out = pl.pallas_call(
        functools.partial(next_kernel, places=places),
        out_shape=out_shape,
        in_specs=[VMEM] * (3 + len(pairs)),
        out_specs=[VMEM] * len(out_shape),
        input_output_aliases={2 + len(pairs): 0},
        compiler_params=PARAMS,
        cost_estimate=attend_cost(query.shape[0], history, query.shape[1]),
    )(query, end, *pairs, total)
    return out if last else out[0]


def after(array, *others):
    return lax.optimization_barrier((array, *others))[0]


def body(
    targets,
    w_query,
    w_gate,
    norm_gain,
    hist_keys,
    hist_values,
    user_offset,
    user_length,
    target_user,
):
    hist_rows = hist_keys.shape[0]
    down, up = ring_perms(lax.axis_size("seq"))
    other_chip = [(0, 2), (2, 0), (1, 3), (3, 1)]
    other_core = [(0, 1), (1, 0), (2, 3), (3, 2)]
    sizes = DOWN + UP
    at = [sum(sizes[:i]) for i in range(len(sizes))]
    chunks = tuple(zip(at, sizes))

    near = lax.ppermute(targets, "tp", other_core)
    a, b = pack(hist_keys, hist_values, chunks)
    far = lax.ppermute(targets, "tp", other_chip)
    a1 = lax.ppermute(a, "seq", down)
    b1 = lax.ppermute(b, "seq", up[0])
    me = lax.axis_index("tp").astype(jnp.int32)
    seq_info = jnp.stack([lax.axis_index("seq").astype(jnp.int32), jnp.int32(hist_rows)])
    start, end = windows(seq_info, user_offset, user_length, target_user)
    partial = project(jnp.stack([me, me ^ 1]), targets, near, w_query, w_gate)
    far, b1 = lax.optimization_barrier((far, b1))
    far_near = lax.ppermute(far, "tp", other_core)
    b2 = lax.ppermute(b1, "seq", up[1])
    a2 = lax.ppermute(a1, "seq", down)
    query, gate = project(jnp.stack([me ^ 2, me ^ 3]), far, far_near, w_query, w_gate, partial)
    total = attend_own(query, start, end, hist_keys, hist_values)
    b3 = lax.ppermute(b2, "seq", up[2])
    one, two = hist_rows, 2 * hist_rows
    total = attend_next(query, end, [(a1, one + at[0])], total)
    total = attend_next(query, end, [(b2, two + at[1])], total)
    total = attend_next(query, end, [(a2, two + at[0])], total)
    attended, stats = attend_next(query, end, [(b3, one + at[1])], total, last=True)

    sums = lax.psum(stats, "tp") / HQ
    mean = sums[0]
    var = sums[1] - mean * mean
    normed = (attended - mean[:, None]) / jnp.sqrt(var[:, None] + 1e-05)
    return (normed * norm_gain[None, :] * gate).astype(jnp.bfloat16)


def solution(mesh):
    return jax.shard_map(
        body,
        mesh=mesh,
        in_specs=(
            P("seq", "tp"),
            P(None, "tp"),
            P(None, "tp"),
            P("tp"),
            P("seq", "tp"),
            P("seq", "tp"),
            P("seq"),
            P("seq"),
            P("seq"),
        ),
        out_specs=P("seq", "tp"),
        check_vma=False,
    )
```
